256 devices in a mesh: chan: 32 (over z_lo, x, core), stn: 8 (over z_hi, y).
Axes of the slice: x: 4, y: 4, z: 8 (z_hi: 2, z_lo: 4; z = z_hi * 4 + z_lo), core: 2. Of those that a mesh axis runs over, the one named last changes fastest.
Arguments:
- samples: bfloat16 [2, 1024, 393216], P(None, 'stn', 'chan'), may hold values from -6 to 6
- chan_index: int32 [512], replicated, may hold values from 0 to 4095, as said below
- flags: int32 [512, 512], P('stn'), may hold values 0 or 1
Outputs:
- visibility: bfloat16 [512, 2, 1024, 640], P('chan', None, 'stn')
The draws below stay inside these ranges and needn't reach their ends.
Inputs may be any that keep to these rules, and one draw needn't show every extreme that they name: `chan_index`: 512 distinct channel numbers; 0 and 4095 are among them.
All inputs are finite; a program needn't handle non-finite values. No bound on the sum of `flags` on one device may be relied on, other than what follows from the above.
Results may differ from the reference program's by a relative error of at most 0.0073.
Values may be sent and summed in bfloat16 or wider, within the bound.
A program may use at most 64 MiB of HBM per device.

```python
import math
import jax
import jax.numpy as jnp
from jax import lax

STATIONS = 512
INPUTS = 1024
DFT_LEN = 4096
TAPS = 4
SPEC_DEV = 3
NSEL = 512
SPECTRA = 96
TIME = 393216
BLOCK = 128
COLBLK = 5
N_STN = 8


def draw_chan_index(key, part):
    first_key, second_key = jax.random.split(jax.random.fold_in(key, 11))
    middle = 1 + jax.random.permutation(first_key, DFT_LEN - 2)[:NSEL - 2]
    chosen = jnp.concatenate([jnp.array([0, DFT_LEN - 1], jnp.int32), middle.astype(jnp.int32)])
    return jax.random.permutation(second_key, chosen)


def set_ends(values, stream_key, least, largest):
    longest = values.shape.index(max(values.shape))
    spots = []
    for shift in (0, 1):
        where = [jax.random.randint(jax.random.fold_in(stream_key, axis), (), 0, length) for axis, length in enumerate(values.shape)]
        where[longest] = (where[longest] + shift) % values.shape[longest]
        spots.append(tuple(where))
    return values.at[spots[0]].set(least).at[spots[1]].set(largest)


def shard_levels(stream_key, extent, shards, least, high):
    gain = 1.0
    for position, parts in shards:
        steps = jax.random.uniform(jax.random.fold_in(jax.random.fold_in(stream_key, 6), position), (parts,), jnp.float32, least / len(shards), high / len(shards))
        gain = gain * jnp.repeat(jnp.exp(steps), extent[position] // parts).reshape((-1,) + (1,) * (len(extent) - 1 - position))
    return gain


def scatter_about(stream_key, dims, spread, reach, cuts=(), kind=jnp.bfloat16):
    level = shard_levels(stream_key, dims, cuts, -0.22, 0.18) if cuts else 1.0
    values = jax.random.normal(stream_key, dims, jnp.float32) * spread * level
    return jnp.minimum(jnp.maximum(values, -reach), reach).astype(kind)


def setup_inputs(seed: int = 0) -> dict:
    splits = jax.random.split(jax.random.key(seed), 4)
    samples = scatter_about(splits[0], (2, INPUTS, TIME), 1.0, 6.0, ((1, 8), (2, 32)))
    chan_index = draw_chan_index(jax.random.fold_in(splits[3], 71), 0)
    flags = set_ends((jax.random.randint(splits[2], (STATIONS, STATIONS), 0, 8) < 1).astype(jnp.int32), jax.random.fold_in(splits[2], 1), 0, 1)
    return {"samples": samples, "chan_index": chan_index, "flags": flags}


def window_table(tap_count, dft_length):
    sample_pos = jnp.arange(tap_count * dft_length, dtype=jnp.float32) + 0.5
    weights = jnp.sinc(sample_pos / dft_length - tap_count / 2.0)
    weights = weights * (0.5 - 0.5 * jnp.cos(2.0 * math.pi / (tap_count * dft_length) * sample_pos))
    weights = weights / jnp.sqrt(jnp.sum(weights * weights))
    return weights.reshape(tap_count, dft_length)

def dft_tables(chan_index, dft_length):
    row_index = jnp.arange(dft_length, dtype=jnp.int32)[:, None]
    phase_index = row_index * chan_index.astype(jnp.int32)[None, :] % dft_length
    angles = phase_index.astype(jnp.float32) * (2.0 * math.pi / dft_length)
    return (jnp.cos(angles).astype(jnp.bfloat16), jnp.sin(angles).astype(jnp.bfloat16))

def reference(samples, chan_index, flags):
    window = window_table(TAPS, DFT_LEN)
    cosine, sine_table = dft_tables(chan_index, DFT_LEN)
    cos_wide = cosine.astype(jnp.float32)
    sin_wide = sine_table.astype(jnp.float32)
    padded = jnp.concatenate([jnp.zeros((2, INPUTS, (TAPS - 1) * DFT_LEN), samples.dtype), samples], axis=2)
    contract = (((0,), (2,)), ((), ()))
    tap_ids = jnp.arange(TAPS, dtype=jnp.int32)

    def transform(frame):
        along_cos = lax.dot_general(cos_wide, frame, contract, precision=lax.Precision.HIGHEST)
        along_sin = lax.dot_general(sin_wide, frame, contract, precision=lax.Precision.HIGHEST)
        return jnp.stack([along_cos[:, 0] + along_sin[:, 1], along_cos[:, 1] - along_sin[:, 0]], axis=1)

    def one_spectrum(spec_index):
        segment = lax.dynamic_slice_in_dim(padded, spec_index * DFT_LEN, TAPS * DFT_LEN, 2)
        segment = segment.reshape(2, INPUTS, TAPS, DFT_LEN).astype(jnp.float32)
        weighted = segment * window[None, None]
        within = spec_index % SPEC_DEV
        carry_mask = (tap_ids < TAPS - 1 - within).astype(jnp.float32)
        carried = lax.optimization_barrier(jnp.sum(weighted * carry_mask[None, None, :, None], axis=2)).astype(jnp.bfloat16).astype(jnp.float32)
        current = lax.optimization_barrier(jnp.sum(weighted * (1.0 - carry_mask)[None, None, :, None], axis=2)).astype(jnp.bfloat16).astype(jnp.float32)
        return (transform(current) + transform(carried)).astype(jnp.bfloat16)
    spectra = lax.map(one_spectrum, jnp.arange(SPECTRA, dtype=jnp.int32))
    block_start = (jnp.arange(N_STN, dtype=jnp.int32)[:, None] - jnp.arange(COLBLK, dtype=jnp.int32)[None, :] + N_STN) % N_STN * BLOCK
    col_rows = (block_start[:, :, None] + jnp.arange(BLOCK, dtype=jnp.int32)[None, None, :]).reshape(N_STN, COLBLK * BLOCK)
    col_full = jnp.repeat(col_rows, BLOCK, axis=0)
    row_full = jnp.arange(INPUTS, dtype=jnp.int32)[:, None]
    keep_mask = (1 - flags[row_full // 2, col_full // 2]).astype(jnp.float32)

    def one_channel(chan):
        chosen = lax.dynamic_index_in_dim(spectra, chan, 1, keepdims=False).astype(jnp.float32)
        swapped = jnp.stack([chosen[:, 1], -chosen[:, 0]], axis=1)
        real_part = jnp.einsum('tra,trb->ab', chosen, chosen, precision=lax.Precision.HIGHEST)
        imag_part = jnp.einsum('tra,trb->ab', swapped, chosen, precision=lax.Precision.HIGHEST)
        full = jnp.stack([real_part, imag_part], axis=0)
        picked = full[:, row_full, col_full]
        return (picked * keep_mask / SPECTRA).astype(jnp.bfloat16)
    return lax.map(one_channel, jnp.arange(NSEL, dtype=jnp.int32))
```

```python
import functools
import math

import jax
import jax.numpy as jnp
import numpy as np
from jax import lax
from jax.experimental import pallas as pl
from jax.experimental.pallas import tpu as pltpu
from jax.sharding import PartitionSpec as P

N = 4096
TAPS = 4

def window_np():
    pos = np.arange(TAPS * N, dtype=np.float64) + 0.5
    w = np.sinc(pos / N - TAPS / 2.0) * (0.5 - 0.5 * np.cos(2.0 * np.pi / (TAPS * N) * pos))
    w = w / np.sqrt(np.sum(w * w))
    return w.reshape(TAPS, N).astype(np.float32)

def cos_sin(q):
    quad = (q + 512) // 1024
    r = (q - quad * 1024).astype(jnp.float32) * (2.0 * math.pi / N)
    z = r * r
    s = r + r * z * (-1.0 / 6 + z * (1.0 / 120 + z * (-1.0 / 5040 + z * (1.0 / 362880))))
    c = 1.0 + z * (-0.5 + z * (1.0 / 24 + z * (-1.0 / 720 + z * (1.0 / 40320))))
    quad = quad & 3
    odd = (quad & 1) == 1
    cc = jnp.where(odd, s, c)
    ss = jnp.where(odd, c, s)
    cc = jnp.where((quad == 1) | (quad == 2), -cc, cc)
    ss = jnp.where(quad >= 2, -ss, ss)
    return cc, ss

ROWS = 64
def make_tables(ci_ref, tc_ref, ts_ref, lanes):
    for lc in lanes:
        for half in range(128 // ROWS):
            k = ci_ref[0:1, lc * 128:(lc + 1) * 128]
            k8 = jnp.broadcast_to(k, (8, 128))
            cd, sd = cos_sin((k8 * 128) & (N - 1))
            b = (lax.broadcasted_iota(jnp.int32, (ROWS // 8, 8, 128), 0) * 8
                 + lax.broadcasted_iota(jnp.int32, (ROWS // 8, 8, 128), 1) + half * ROWS)
            c, s = cos_sin((b * k8[None]) & (N - 1))
            def step(i, cs):
                c, s = cs
                row = pl.ds(pl.multiple_of(i * 128 + half * ROWS, ROWS), ROWS)
                tc_ref[row, lc * 128:(lc + 1) * 128] = c.reshape(ROWS, 128).astype(jnp.bfloat16)
                ts_ref[row, lc * 128:(lc + 1) * 128] = s.reshape(ROWS, 128).astype(jnp.bfloat16)
                return c * cd[None] - s * sd[None], s * cd[None] + c * sd[None]
            lax.fori_loop(0, N // 128, step, (c, s), unroll=2)

FT = 32
def make_frames(win_ref, x_ref, f_ref):
    def step(i, _):
        m0 = pl.multiple_of(i * 128, 128)
        w = [win_ref[p:p + 1, pl.ds(m0, 128)] for p in range(4)]
        for r in range(2):
            for a in range(0, 128, FT):
                x = [x_ref[r, a:a + FT, pl.ds(pl.multiple_of(t * N + m0, 128), 128)].astype(jnp.float32) for t in range(3)]
                o = [w[3] * x[0], w[2] * x[0] + w[3] * x[1], w[1] * x[0] + w[2] * x[1] + w[3] * x[2],
                     w[0] * x[0] + w[1] * x[1] + w[2] * x[2], w[0] * x[1] + w[1] * x[2], w[0] * x[2]]
                for u in range(6):
                    f_ref[u, r * 128 + a:r * 128 + a + FT, pl.ds(m0, 128)] = o[u].astype(jnp.bfloat16)
        return 0
    lax.fori_loop(0, N // 128, step, 0)

def dft(f_ref, tc_ref, ts_ref, us, n0, nw):
    l = f_ref[us, :, :].reshape(-1, N) if not isinstance(us, int) else f_ref[us]
    pc = jnp.dot(l, tc_ref[:, n0:n0 + nw], preferred_element_type=jnp.float32)
    ps = jnp.dot(l, ts_ref[:, n0:n0 + nw], preferred_element_type=jnp.float32)
    return pc, ps

def kernel1(NU, NW, ci_ref, win_ref, x_hbm, main_ref, carry_ref, x_ref, f_ref, tc_ref, ts_ref, sem):
    cp = pltpu.make_async_copy(x_hbm, x_ref, sem)
    cp.start()
    make_tables(ci_ref, tc_ref, ts_ref, range(4))
    cp.wait()
    make_frames(win_ref, x_ref, f_ref)
    for n0 in range(0, 512, NW):
        def body(ui, _):
            us = pl.ds(ui * NU, NU)
            pc, ps = dft(f_ref, tc_ref, ts_ref, us, n0, NW)
            pc = pc.reshape(NU, 2, 128, NW); ps = ps.reshape(NU, 2, 128, NW)
            re = pc[:, 0] + ps[:, 1]; im = pc[:, 1] - ps[:, 0]
            @pl.when(ui * NU < 3)
            def _():
                for j in range(NU):
                    main_ref[0, ui * NU + j, :, n0:n0 + NW] = re[j]
                    main_ref[1, ui * NU + j, :, n0:n0 + NW] = im[j]
            @pl.when(ui * NU >= 3)
            def _():
                for j in range(NU):
                    carry_ref[0, ui * NU + j - 3, :, n0:n0 + NW] = re[j].astype(jnp.bfloat16)
                    carry_ref[1, ui * NU + j - 3, :, n0:n0 + NW] = im[j].astype(jnp.bfloat16)
            return 0
        lax.fori_loop(0, 6 // NU, body, 0)

def call1(ci, win, x, NU=1, NW=256):
    V = pl.BlockSpec(memory_space=pltpu.VMEM)
    return pl.pallas_call(
        functools.partial(kernel1, NU, NW),
        out_shape=(jax.ShapeDtypeStruct((2, 3, 128, 512), jnp.float32), jax.ShapeDtypeStruct((2, 3, 128, 512), jnp.bfloat16)),
        in_specs=[V, V, pl.BlockSpec(memory_space=pl.ANY)],
        out_specs=(V, V),
        scratch_shapes=[pltpu.VMEM((2, 128, 3 * N), jnp.bfloat16), pltpu.VMEM((6, 256, N), jnp.bfloat16),
                        pltpu.VMEM((N, 512), jnp.bfloat16), pltpu.VMEM((N, 512), jnp.bfloat16), pltpu.SemaphoreType.DMA],
        compiler_params=pltpu.CompilerParams(vmem_limit_bytes=56 * 2**20),
    )(ci.reshape(1, 512), win, x)
MESH = pl.DeviceIdType.MESH

def signal(sem, dest):
    pl.semaphore_signal(sem, inc=1, device_id=dest, device_id_type=MESH)

def kernel2(main_ref, carry_ref, g_ref, cin_ref, p_ref, send_sem, csend, crecv, zrecv, ysend, yrecv):
    chan, stn = lax.axis_index("chan"), lax.axis_index("stn")
    zl, x, core = chan // 8, (chan // 2) % 4, chan % 2
    zh, y = stn // 4, stn % 4
    z = zh * 4 + zl

    def peer(i):
        dz, dx, dc = i // 8, (i // 2) % 4, i % 2
        zz = (z + dz) % 8
        return (zz % 4) * 8 + ((x + dx) % 4) * 2 + (core + dc) % 2, (zz // 4) * 4 + y

    barrier = pltpu.get_barrier_semaphore()
    def greet(i, _):
        signal(barrier, peer(i))
        return 0
    lax.fori_loop(1, 64, greet, 0)
    def greet_y(d, _):
        signal(barrier, (chan, zh * 4 + (y + d) % 4))
        return 0
    lax.fori_loop(1, 4, greet_y, 0)
    pl.semaphore_wait(barrier, 66)

    def carry_copy(dest):
        return pltpu.make_async_remote_copy(src_ref=carry_ref, dst_ref=cin_ref, send_sem=csend, recv_sem=crecv,
                                            device_id=(dest, stn), device_id_type=MESH)
    @pl.when(chan < 31)
    def _():
        carry_copy(chan + 1).start()
    @pl.when(chan == 0)
    def _():
        cin_ref[...] = jnp.zeros_like(cin_ref)
    @pl.when(chan > 0)
    def _():
        carry_copy(chan).wait_recv()

    for k in range(6):
        full = main_ref[k // 3, k % 3] + cin_ref[k // 3, k % 3].astype(jnp.float32)
        for cb in range(4):
            blk = full[:, cb * 128:(cb + 1) * 128].T.astype(jnp.bfloat16)
            p_ref[cb * 8:(cb + 1) * 8, k * 16:(k + 1) * 16, :] = blk.reshape(8, 16, 128)

    def piece(i):
        c2, s2 = peer(i)
        return pltpu.make_async_remote_copy(
            src_ref=p_ref.at[c2], dst_ref=g_ref.at[4 * jnp.where(s2 == stn, 0, 1), chan],
            send_sem=send_sem, recv_sem=zrecv.at[z], device_id=(c2, s2), device_id_type=MESH)
    own = pltpu.make_async_copy(p_ref.at[chan], g_ref.at[0, chan], zrecv.at[z])
    own.start()
    def send(n, _):
        h = n // 8
        dz = 4 + jnp.where(h % 2 == 0, h // 2, 0 - (h + 1) // 2)
        dz = (4 + (1 - 2 * (h % 2)) * ((h + 1) // 2)) % 8
        piece(dz * 8 + n % 8).start()
        return 0
    lax.fori_loop(0, 56, send, 0)
    def send0(n, _):
        piece(n).start()
        return 0
    lax.fori_loop(1, 8, send0, 0)

    def zwait(j, zg):
        v = g_ref.at[j, pl.ds((zg % 4) * 8, 8)]
        pltpu.make_async_copy(v, v, zrecv.at[zg]).wait()

    def ycopy(d, zz):
        jsrc = jnp.where(y + d < 4, 0, 4)
        return pltpu.make_async_remote_copy(
            src_ref=g_ref.at[jsrc, pl.ds(zz * 8, 8)], dst_ref=g_ref.at[d, pl.ds(zz * 8, 8)],
            send_sem=ysend, recv_sem=yrecv.at[d], device_id=(chan, zh * 4 + (y + d) % 4), device_id_type=MESH)
    def relay(q, _):
        zz = (zl + q) % 4
        zwait(0, zh * 4 + zz)
        zwait(4, (1 - zh) * 4 + zz)
        for d in (2, 1, 3):
            ycopy(d, zz).start()
        return 0
    lax.fori_loop(0, 4, relay, 0)
    for d in (1, 2, 3):
        v = g_ref.at[d]
        pltpu.make_async_copy(v, v, yrecv.at[d]).wait()
    v = g_ref.at[pl.ds(1, 3)]
    pltpu.make_async_copy(v, v, ysend).wait()
    v = p_ref.at[pl.ds(0, 31)]
    w = p_ref
    pltpu.make_async_copy(g_ref.at[pl.ds(0, 2), pl.ds(0, 31)], g_ref.at[pl.ds(0, 2), pl.ds(0, 31)], send_sem).wait()
    pltpu.make_async_copy(p_ref.at[0], p_ref.at[0], send_sem).wait()
    @pl.when(chan < 31)
    def _():
        carry_copy(chan + 1).wait_send()

def call2(main, carry):
    V = pl.BlockSpec(memory_space=pltpu.VMEM)
    D = pltpu.SemaphoreType.DMA
    return pl.pallas_call(
        kernel2, out_shape=jax.ShapeDtypeStruct((5, 32, 96, 128), jnp.bfloat16),
        in_specs=[V, V], out_specs=V,
        scratch_shapes=[pltpu.VMEM((2, 3, 128, 512), jnp.bfloat16), pltpu.VMEM((32, 96, 128), jnp.bfloat16),
                        D, D, D, D((8,)), D, D((4,))],
        compiler_params=pltpu.CompilerParams(collective_id=0, has_side_effects=True, vmem_limit_bytes=40 * 2**20),
    )(main, carry)

def kernel3(g_ref, mask_ref, out_ref, f_ref, y_ref):
    @pl.when(pl.program_id(0) == 0)
    def _():
        for j in range(5):
            def conv(s, _):
                f_ref[pl.ds(pl.multiple_of(s * 96, 96), 96), :] = g_ref[j, s].astype(jnp.float32)
                return 0
            lax.fori_loop(0, 32, conv, 0, unroll=4)
            for c in range(16):
                for k in range(6):
                    y_ref[c, k * 32:(k + 1) * 32, j * 128:(j + 1) * 128] = f_ref[pl.ds(k * 16 + c, 32, stride=96), :].astype(jnp.bfloat16)
    m = mask_ref[...]
    for i in range(4):
        c = pl.program_id(0) * 4 + i
        yv = y_ref[c]
        xv = yv[:, :128]
        sv = jnp.concatenate([xv[96:], -xv[:96]], axis=0)
        ct = (((0,), (0,)), ((), ()))
        out_ref[i, 0] = (lax.dot_general(xv, yv, ct, preferred_element_type=jnp.float32) * m).astype(jnp.bfloat16)
        out_ref[i, 1] = (lax.dot_general(sv, yv, ct, preferred_element_type=jnp.float32) * m).astype(jnp.bfloat16)

def call3(g, mask):
    return pl.pallas_call(
        kernel3, grid=(4,), out_shape=jax.ShapeDtypeStruct((16, 2, 128, 640), jnp.bfloat16),
        in_specs=[pl.BlockSpec((5, 32, 96, 128), lambda i: (0, 0, 0, 0)), pl.BlockSpec((128, 640), lambda i: (0, 0))],
        out_specs=pl.BlockSpec((4, 2, 128, 640), lambda i: (i, 0, 0, 0)),
        scratch_shapes=[pltpu.VMEM((32 * 96, 128), jnp.float32), pltpu.VMEM((16, 192, 640), jnp.bfloat16)],
        compiler_params=pltpu.CompilerParams(vmem_limit_bytes=40 * 2**20),
    )(g, mask)
def keep(flags):
    own = lax.axis_index("stn")
    strips = [lax.dynamic_slice_in_dim(flags, (own - o + 8) % 8 * 64, 64, 1) for o in range(5)]
    m = (1 - jnp.concatenate(strips, axis=1)).astype(jnp.float32) / 96
    return jnp.repeat(jnp.repeat(m, 2, axis=0), 2, axis=1)
def on_device(samples, chan_index, flags):
    main, carry = call1(chan_index, jnp.asarray(window_np()), samples, 3, 256)
    g = call2(main, carry)
    return call3(g, keep(flags))
def solution(mesh):
    return jax.shard_map(on_device, mesh=mesh, in_specs=(P(None, "stn", "chan"), P(), P("stn", None)), out_specs=P("chan", None, "stn", None), check_vma=False)
```

```python
import functools
import math

import jax
import jax.numpy as jnp
import numpy as np
from jax import lax
from jax.experimental import pallas as pl
from jax.experimental.pallas import tpu as pltpu
from jax.sharding import PartitionSpec as P

N = 4096
TAPS = 4

def window_np():
    pos = np.arange(TAPS * N, dtype=np.float64) + 0.5
    w = np.sinc(pos / N - TAPS / 2.0) * (0.5 - 0.5 * np.cos(2.0 * np.pi / (TAPS * N) * pos))
    w = w / np.sqrt(np.sum(w * w))
    return w.reshape(TAPS, N).astype(np.float32)

def cos_sin(q):
    quad = (q + 512) // 1024
    r = (q - quad * 1024).astype(jnp.float32) * (2.0 * math.pi / N)
    z = r * r
    s = r + r * z * (-1.0 / 6 + z * (1.0 / 120 + z * (-1.0 / 5040 + z * (1.0 / 362880))))
    c = 1.0 + z * (-0.5 + z * (1.0 / 24 + z * (-1.0 / 720 + z * (1.0 / 40320))))
    quad = quad & 3
    odd = (quad & 1) == 1
    cc = jnp.where(odd, s, c)
    ss = jnp.where(odd, c, s)
    cc = jnp.where((quad == 1) | (quad == 2), -cc, cc)
    ss = jnp.where(quad >= 2, -ss, ss)
    return cc, ss

ROWS = 64
def make_tables(ci_ref, tc_ref, ts_ref, lanes):
    for lc in lanes:
        for half in range(128 // ROWS):
            k = ci_ref[0:1, lc * 128:(lc + 1) * 128]
            k8 = jnp.broadcast_to(k, (8, 128))
            cd, sd = cos_sin((k8 * 128) & (N - 1))
            b = (lax.broadcasted_iota(jnp.int32, (ROWS // 8, 8, 128), 0) * 8
                 + lax.broadcasted_iota(jnp.int32, (ROWS // 8, 8, 128), 1) + half * ROWS)
            c, s = cos_sin((b * k8[None]) & (N - 1))
            def step(i, cs):
                c, s = cs
                row = pl.ds(pl.multiple_of(i * 128 + half * ROWS, ROWS), ROWS)
                tc_ref[row, lc * 128:(lc + 1) * 128] = c.reshape(ROWS, 128).astype(jnp.bfloat16)
                ts_ref[row, lc * 128:(lc + 1) * 128] = s.reshape(ROWS, 128).astype(jnp.bfloat16)
                return c * cd[None] - s * sd[None], s * cd[None] + c * sd[None]
            lax.fori_loop(0, N // 128, step, (c, s), unroll=2)

FT = 32
MESH = pl.DeviceIdType.MESH
UNITS = (2, 1, 0)

def signal(sem, dest):
    pl.semaphore_signal(sem, inc=1, device_id=dest, device_id_type=MESH)

def make_unit_frames(u, win_ref, x_ref, f_ref):
    def step(i, _):
        m0 = pl.multiple_of(i * 128, 128)
        w = [win_ref[p:p + 1, pl.ds(m0, 128)] for p in range(4)]
        for r in range(2):
            for a in range(0, 128, FT):
                x = [x_ref[r, a:a + FT, pl.ds(pl.multiple_of(t * N + m0, 128), 128)].astype(jnp.float32) for t in range(3)]
                cur = sum(w[3 - u + t] * x[t] for t in range(u + 1))
                car = sum(w[t - u] * x[t] for t in range(u, 3))
                row = slice(r * 128 + a, r * 128 + a + FT)
                f_ref[0, row, pl.ds(m0, 128)] = car.astype(jnp.bfloat16)
                f_ref[1, row, pl.ds(m0, 128)] = cur.astype(jnp.bfloat16)
        return 0
    lax.fori_loop(0, N // 128, step, 0)

def half_dft(frame, tc_ref, ts_ref, n0, nw):
    pc = jnp.dot(frame, tc_ref[:, n0:n0 + nw], preferred_element_type=jnp.float32)
    ps = jnp.dot(frame, ts_ref[:, n0:n0 + nw], preferred_element_type=jnp.float32)
    return pc[:128] + ps[128:], pc[128:] - ps[:128]

def exchange_kernel(ci_ref, win_ref, x_hbm, g_ref, x_ref, f_ref, tc_ref, ts_ref, main_ref, cout_ref, cin_ref, p_ref,
                    xsem, csend, crecv, zsend, zrecv, ysend, yrecv):
    chan, stn = lax.axis_index("chan"), lax.axis_index("stn")
    zl, x, core = chan // 8, (chan // 2) % 4, chan % 2
    zh, y = stn // 4, stn % 4
    late = y // 2

    xcopy = pltpu.make_async_copy(x_hbm, x_ref, xsem)
    xcopy.start()

    barrier = pltpu.get_barrier_semaphore()
    def peer(n):
        far = (n // 32 + late) % 2
        q = (n // 8) % 4
        zz = (zl + 4 - q) % 4
        return zz * 8 + ((x + (n // 2) % 4) % 4) * 2 + (core + n) % 2, ((zh + far) % 2) * 4 + y, far
    def greet(n, _):
        c2, s2, far = peer(n)
        @pl.when(jnp.logical_or(c2 != chan, s2 != stn))
        def _():
            signal(barrier, (c2, s2))
        return 0
    lax.fori_loop(0, 64, greet, 0)
    def greet_y(d, _):
        signal(barrier, (chan, zh * 4 + (y + d) % 4))
        return 0
    lax.fori_loop(1, 4, greet_y, 0)

    make_tables(ci_ref, tc_ref, ts_ref, range(4))
    xcopy.wait()

    def carry_copy(u, dest):
        return pltpu.make_async_remote_copy(src_ref=cout_ref.at[u], dst_ref=cin_ref.at[u], send_sem=csend.at[u],
                                            recv_sem=crecv.at[u], device_id=(dest, stn), device_id_type=MESH)

    def send_pieces(u):
        pltpu.make_async_copy(p_ref.at[u, chan], g_ref.at[0, u, chan], zrecv.at[u, zh * 4 + zl]).start()
        def send(n, _):
            c2, s2, far = peer(n)
            @pl.when(jnp.logical_or(c2 != chan, s2 != stn))
            def _():
                pltpu.make_async_remote_copy(
                    src_ref=p_ref.at[u, c2], dst_ref=g_ref.at[4 * far, u, chan], send_sem=zsend,
                    recv_sem=zrecv.at[u, zh * 4 + zl], device_id=(c2, s2), device_id_type=MESH).start()
            return 0
        lax.fori_loop(0, 64, send, 0)

    def forward(u, first, last):
        def group(n, _):
            far = (n // 4 + late) % 2
            zz = (zl + n) % 4
            v = g_ref.at[4 * far, u, pl.ds(zz * 8, 8)]
            pltpu.make_async_copy(v, v, zrecv.at[u, ((zh + far) % 2) * 4 + zz]).wait()
            for d in (2, 1, 3):
                @pl.when((y + d) // 4 == far)
                def _():
                    pltpu.make_async_remote_copy(
                        src_ref=g_ref.at[4 * far, u, pl.ds(zz * 8, 8)], dst_ref=g_ref.at[d, u, pl.ds(zz * 8, 8)],
                        send_sem=ysend, recv_sem=yrecv.at[u], device_id=(chan, zh * 4 + (y + d) % 4),
                        device_id_type=MESH).start()
            return 0
        lax.fori_loop(first, last, group, 0)

    for i, u in enumerate(UNITS):
        make_unit_frames(u, win_ref, x_ref, f_ref)
        for n0 in range(0, 512, NW):
            re, im = half_dft(f_ref[0], tc_ref, ts_ref, n0, NW)
            cout_ref[u, 0, :, n0:n0 + NW] = re.astype(jnp.bfloat16)
            cout_ref[u, 1, :, n0:n0 + NW] = im.astype(jnp.bfloat16)
        if i == 0:
            pl.semaphore_wait(barrier, 66)
        @pl.when(chan < 31)
        def _():
            carry_copy(u, chan + 1).start()
        for n0 in range(0, 512, NW):
            re, im = half_dft(f_ref[1], tc_ref, ts_ref, n0, NW)
            main_ref[0, :, n0:n0 + NW] = re
            main_ref[1, :, n0:n0 + NW] = im
        @pl.when(chan == 0)
        def _():
            cin_ref[u] = jnp.zeros((2, 128, 512), jnp.bfloat16)
        @pl.when(chan > 0)
        def _():
            carry_copy(u, chan).wait_recv()
        for r in range(2):
            full = main_ref[r] + cin_ref[u, r].astype(jnp.float32)
            for cb in range(4):
                blk = full[:, cb * 128:(cb + 1) * 128].T.astype(jnp.bfloat16)
                p_ref[u, cb * 8:(cb + 1) * 8, r * 16:(r + 1) * 16, :] = blk.reshape(8, 16, 128)
        send_pieces(u)
        if i == 1:
            forward(UNITS[0], 0, 4)
    forward(UNITS[0], 4, 8)
    forward(UNITS[1], 0, 8)
    forward(UNITS[2], 0, 8)
    for u in UNITS:
        v = g_ref.at[pl.ds(1, 3), u]
        pltpu.make_async_copy(v, v, yrecv.at[u]).wait()
    for u in UNITS:
        v = g_ref.at[pl.ds(1, 3), u]
        pltpu.make_async_copy(v, v, ysend).wait()
        v = g_ref.at[pl.ds(0, 2), u, pl.ds(0, 31)]
        pltpu.make_async_copy(v, v, zsend).wait()
        v = p_ref.at[u, 0]
        pltpu.make_async_copy(v, v, zsend).wait()
        @pl.when(chan < 31)
        def _():
            carry_copy(u, chan + 1).wait_send()

NW = 256
def exchange(ci, win, x):
    V = pl.BlockSpec(memory_space=pltpu.VMEM)
    D = pltpu.SemaphoreType.DMA
    bf = jnp.bfloat16
    return pl.pallas_call(
        exchange_kernel, out_shape=jax.ShapeDtypeStruct((5, 3, 32, 32, 128), bf),
        in_specs=[V, V, pl.BlockSpec(memory_space=pl.ANY)], out_specs=V,
        scratch_shapes=[pltpu.VMEM((2, 128, 3 * N), bf), pltpu.VMEM((2, 256, N), bf), pltpu.VMEM((N, 512), bf), pltpu.VMEM((N, 512), bf),
                        pltpu.VMEM((2, 128, 512), jnp.float32), pltpu.VMEM((3, 2, 128, 512), bf), pltpu.VMEM((3, 2, 128, 512), bf),
                        pltpu.VMEM((3, 32, 32, 128), bf),
                        D, D((3,)), D((3,)), D, D((3, 8)), D, D((3,))],
        compiler_params=pltpu.CompilerParams(collective_id=0, has_side_effects=True, vmem_limit_bytes=52 * 2**20),
    )(ci.reshape(1, 512), win, x)

def correlate_kernel(g_ref, mask_ref, out_ref, gv_ref, f_ref, y_ref, sem):
    @pl.when(pl.program_id(0) == 0)
    def _():
        copies = [pltpu.make_async_copy(g_ref.at[j], gv_ref.at[j], sem.at[j]) for j in range(5)]
        for c in copies:
            c.start()
        for j in range(5):
            copies[j].wait()
            for u in range(3):
                f_ref[u * 1024:(u + 1) * 1024, :] = gv_ref[j, u].reshape(1024, 128).astype(jnp.float32)
            for c in range(16):
                for r in range(2):
                    for u in range(3):
                        k = r * 3 + u
                        y_ref[c, k * 32:(k + 1) * 32, j * 128:(j + 1) * 128] = (
                            f_ref[pl.ds(u * 1024 + r * 16 + c, 32, stride=32), :].astype(jnp.bfloat16))
    m = mask_ref[...]
    for i in range(4):
        c = pl.program_id(0) * 4 + i
        yv = y_ref[c]
        xv = yv[:, :128]
        sv = jnp.concatenate([xv[96:], -xv[:96]], axis=0)
        ct = (((0,), (0,)), ((), ()))
        out_ref[i, 0] = (lax.dot_general(xv, yv, ct, preferred_element_type=jnp.float32) * m).astype(jnp.bfloat16)
        out_ref[i, 1] = (lax.dot_general(sv, yv, ct, preferred_element_type=jnp.float32) * m).astype(jnp.bfloat16)

def correlate(g, mask):
    return pl.pallas_call(
        correlate_kernel, grid=(4,), out_shape=jax.ShapeDtypeStruct((16, 2, 128, 640), jnp.bfloat16),
        in_specs=[pl.BlockSpec(memory_space=pl.ANY), pl.BlockSpec((128, 640), lambda i: (0, 0))],
        out_specs=pl.BlockSpec((4, 2, 128, 640), lambda i: (i, 0, 0, 0)),
        scratch_shapes=[pltpu.VMEM((5, 3, 32, 32, 128), jnp.bfloat16), pltpu.VMEM((3072, 128), jnp.float32),
                        pltpu.VMEM((16, 192, 640), jnp.bfloat16), pltpu.SemaphoreType.DMA((5,))],
        compiler_params=pltpu.CompilerParams(vmem_limit_bytes=40 * 2**20),
    )(g, mask)
def keep_factor(flags):
    own = lax.axis_index("stn")
    strips = [lax.dynamic_slice_in_dim(flags, (own - o + 8) % 8 * 64, 64, 1) for o in range(5)]
    m = (1 - jnp.concatenate(strips, axis=1)).astype(jnp.float32) / 96
    return jnp.repeat(jnp.repeat(m, 2, axis=0), 2, axis=1)

def on_device(samples, chan_index, flags):
    g = exchange(chan_index, jnp.asarray(window_np()), samples)
    return correlate(g, keep_factor(flags))

def solution(mesh):
    return jax.shard_map(on_device, mesh=mesh, in_specs=(P(None, "stn", "chan"), P(), P("stn", None)),
                         out_specs=P("chan", None, "stn", None), check_vma=False)
```

```python
import functools
import math

import jax
import jax.numpy as jnp
import numpy as np
from jax import lax
from jax.experimental import pallas as pl
from jax.experimental.pallas import tpu as pltpu
from jax.sharding import PartitionSpec as P

N = 4096
TAPS = 4

def window_np():
    pos = np.arange(TAPS * N, dtype=np.float64) + 0.5
    w = np.sinc(pos / N - TAPS / 2.0) * (0.5 - 0.5 * np.cos(2.0 * np.pi / (TAPS * N) * pos))
    w = w / np.sqrt(np.sum(w * w))
    return w.reshape(TAPS, N).astype(np.float32)

def cos_sin(q):
    quad = (q + 512) // 1024
    r = (q - quad * 1024).astype(jnp.float32) * (2.0 * math.pi / N)
    z = r * r
    s = r + r * z * (-1.0 / 6 + z * (1.0 / 120 + z * (-1.0 / 5040 + z * (1.0 / 362880))))
    c = 1.0 + z * (-0.5 + z * (1.0 / 24 + z * (-1.0 / 720 + z * (1.0 / 40320))))
    quad = quad & 3
    odd = (quad & 1) == 1
    cc = jnp.where(odd, s, c)
    ss = jnp.where(odd, c, s)
    cc = jnp.where((quad == 1) | (quad == 2), -cc, cc)
    ss = jnp.where(quad >= 2, -ss, ss)
    return cc, ss

ROWS = 64
def make_tables(ci_ref, tc_ref, ts_ref, lanes):
    for lc in lanes:
        for half in range(128 // ROWS):
            k = ci_ref[0:1, lc * 128:(lc + 1) * 128]
            k8 = jnp.broadcast_to(k, (8, 128))
            cd, sd = cos_sin((k8 * 128) & (N - 1))
            b = (lax.broadcasted_iota(jnp.int32, (ROWS // 8, 8, 128), 0) * 8
                 + lax.broadcasted_iota(jnp.int32, (ROWS // 8, 8, 128), 1) + half * ROWS)
            c, s = cos_sin((b * k8[None]) & (N - 1))
            def step(i, cs):
                c, s = cs
                row = pl.ds(pl.multiple_of(i * 128 + half * ROWS, ROWS), ROWS)
                tc_ref[row, lc * 128:(lc + 1) * 128] = c.reshape(ROWS, 128).astype(jnp.bfloat16)
                ts_ref[row, lc * 128:(lc + 1) * 128] = s.reshape(ROWS, 128).astype(jnp.bfloat16)
                return c * cd[None] - s * sd[None], s * cd[None] + c * sd[None]
            lax.fori_loop(0, N // 128, step, (c, s), unroll=2)

FT = 32
MESH = pl.DeviceIdType.MESH
UNITS = (2, 1, 0)

def signal(sem, dest):
    pl.semaphore_signal(sem, inc=1, device_id=dest, device_id_type=MESH)

def make_frames(u, carried, win_ref, x_ref, f_ref):
    def step(i, _):
        m0 = pl.multiple_of(i * 128, 128)
        w = [win_ref[p:p + 1, pl.ds(m0, 128)] for p in range(4)]
        segments = range(u, 3) if carried else range(u + 1)
        for r in range(2):
            for a in range(0, 128, FT):
                frame = 0.0
                for t in segments:
                    x = x_ref[r, a:a + FT, pl.ds(pl.multiple_of(t * N + m0, 128), 128)].astype(jnp.float32)
                    frame = frame + w[t - u if carried else 3 - u + t] * x
                f_ref[r * 128 + a:r * 128 + a + FT, pl.ds(m0, 128)] = frame.astype(jnp.bfloat16)
        return 0
    lax.fori_loop(0, N // 128, step, 0)

def relayout(j, u, g_ref, wide_ref, y_ref):
    lanes = pl.ds(pl.multiple_of(j * 128, 128), 128)
    wide_ref[...] = g_ref[j, u].reshape(1024, 128).astype(jnp.float32)
    for c in range(16):
        for r in range(2):
            k = (r * 3 + u) * 32
            y_ref[c, k:k + 32, lanes] = wide_ref[pl.ds(r * 16 + c, 32, stride=32), :].astype(jnp.bfloat16)

def half_dft(frame, tc_ref, ts_ref, n0, nw):
    pc = jnp.dot(frame, tc_ref[:, n0:n0 + nw], preferred_element_type=jnp.float32)
    ps = jnp.dot(frame, ts_ref[:, n0:n0 + nw], preferred_element_type=jnp.float32)
    return pc[:128] + ps[128:], pc[128:] - ps[:128]

def exchange_kernel(ci_ref, win_hbm, x_hbm, y_ref, g_ref, wide_ref, win_ref, x_ref, f_ref, tc_ref, ts_ref, main_ref, cout_ref, cin_ref, p_ref,
                    xsem, wsem, csend, crecv, zsend, zrecv, ysend, yrecv):
    chan, stn = lax.axis_index("chan"), lax.axis_index("stn")
    zl, x, core = chan // 8, (chan // 2) % 4, chan % 2
    zh, y = stn // 4, stn % 4
    late = y // 2

    xcopy = pltpu.make_async_copy(x_hbm, x_ref, xsem)
    xcopy.start()
    wcopy = pltpu.make_async_copy(win_hbm, win_ref, wsem)
    wcopy.start()

    barrier = pltpu.get_barrier_semaphore()
    def peer(n):
        far = (n // 32 + late) % 2
        q = (n // 8) % 4
        zz = (zl + 4 - q) % 4
        return zz * 8 + ((x + (n // 2) % 4) % 4) * 2 + (core + n) % 2, ((zh + far) % 2) * 4 + y, far
    def greet(n, _):
        c2, s2, far = peer(n)
        @pl.when(jnp.logical_or(c2 != chan, s2 != stn))
        def _():
            signal(barrier, (c2, s2))
        return 0
    lax.fori_loop(0, 64, greet, 0)
    def greet_y(d, _):
        signal(barrier, (chan, zh * 4 + (y + d) % 4))
        return 0
    lax.fori_loop(1, 4, greet_y, 0)

    make_tables(ci_ref, tc_ref, ts_ref, range(4))
    wcopy.wait()
    xcopy.wait()

    def carry_copy(u, dest):
        return pltpu.make_async_remote_copy(src_ref=cout_ref.at[u], dst_ref=cin_ref.at[u], send_sem=csend.at[u],
                                            recv_sem=crecv.at[u], device_id=(dest, stn), device_id_type=MESH)

    def keep_own(u):
        pltpu.make_async_copy(p_ref.at[u, chan], g_ref.at[0, u, chan], zrecv.at[u, zh * 4 + zl]).start()

    def send_batch(u, b):
        def send(n, _):
            c2, s2, far = peer(n)
            @pl.when(jnp.logical_or(c2 != chan, s2 != stn))
            def _():
                pltpu.make_async_remote_copy(
                    src_ref=p_ref.at[u, c2], dst_ref=g_ref.at[4 * far, u, chan], send_sem=zsend,
                    recv_sem=zrecv.at[u, zh * 4 + zl], device_id=(c2, s2), device_id_type=MESH).start()
            return 0
        lax.fori_loop(b * 8, b * 8 + 8, send, 0)

    def forward(u, n):
        far = (n // 4 + late) % 2
        zz = (zl + n) % 4
        v = g_ref.at[4 * far, u, pl.ds(zz * 8, 8)]
        pltpu.make_async_copy(v, v, zrecv.at[u, ((zh + far) % 2) * 4 + zz]).wait()
        for d in (2, 1, 3):
            @pl.when((y + d) // 4 == far)
            def _():
                pltpu.make_async_remote_copy(
                    src_ref=g_ref.at[4 * far, u, pl.ds(zz * 8, 8)], dst_ref=g_ref.at[d, u, pl.ds(zz * 8, 8)],
                    send_sem=ysend, recv_sem=yrecv.at[u], device_id=(chan, zh * 4 + (y + d) % 4),
                    device_id_type=MESH).start()

    def carried_part(u):
        make_frames(u, True, win_ref, x_ref, f_ref)
        for n0 in range(0, 512, NW):
            re, im = half_dft(f_ref[...], tc_ref, ts_ref, n0, NW)
            cout_ref[u, 0, :, n0:n0 + NW] = re.astype(jnp.bfloat16)
            cout_ref[u, 1, :, n0:n0 + NW] = im.astype(jnp.bfloat16)
        if u == UNITS[0]:
            pl.semaphore_wait(barrier, 66)
        @pl.when(chan < 31)
        def _():
            carry_copy(u, chan + 1).start()

    def current_part(u):
        make_frames(u, False, win_ref, x_ref, f_ref)
        for n0 in range(0, 512, NW):
            re, im = half_dft(f_ref[...], tc_ref, ts_ref, n0, NW)
            main_ref[0, :, n0:n0 + NW] = re
            main_ref[1, :, n0:n0 + NW] = im

    def pieces(u):
        @pl.when(chan == 0)
        def _():
            cin_ref[u] = jnp.zeros((2, 128, 512), jnp.bfloat16)
        @pl.when(chan > 0)
        def _():
            carry_copy(u, chan).wait_recv()
        for r in range(2):
            full = main_ref[r] + cin_ref[u, r].astype(jnp.float32)
            for cb in range(4):
                blk = full[:, cb * 128:(cb + 1) * 128].T.astype(jnp.bfloat16)
                p_ref[u, cb * 8:(cb + 1) * 8, r * 16:(r + 1) * 16, :] = blk.reshape(8, 16, 128)
        keep_own(u)

    def own_blocks(u):
        relayout(0, u, g_ref, wide_ref, y_ref)
        relayout(4, u, g_ref, wide_ref, y_ref)

    def other_blocks(u):
        v = g_ref.at[pl.ds(1, 3), u]
        pltpu.make_async_copy(v, v, yrecv.at[u]).wait()
        for j in range(1, 4):
            relayout(j, u, g_ref, wide_ref, y_ref)

    def steps(before, after, start, stop):
        def step(n, _):
            if before is not None:
                forward(before, n)
            if after is not None:
                send_batch(after, n)
            return 0
        lax.fori_loop(start, stop, step, 0)

    first, second, third = UNITS
    carried_part(first)
    current_part(first)
    pieces(first)
    steps(None, first, 0, 4)
    carried_part(second)
    steps(None, first, 4, 8)
    current_part(second)
    steps(first, None, 0, 3)
    carried_part(third)
    steps(first, None, 3, 5)
    pieces(second)
    steps(None, second, 0, 4)
    current_part(third)
    steps(first, None, 5, 6)
    steps(first, second, 6, 8)
    steps(None, second, 4, 6)
    pieces(third)
    steps(second, third, 0, 8)
    own_blocks(first)
    own_blocks(second)
    steps(third, None, 0, 8)
    other_blocks(first)
    own_blocks(third)
    other_blocks(second)
    other_blocks(third)
    for u in UNITS:
        v = g_ref.at[pl.ds(1, 3), u]
        pltpu.make_async_copy(v, v, ysend).wait()
        v = g_ref.at[pl.ds(0, 2), u, pl.ds(0, 31)]
        pltpu.make_async_copy(v, v, zsend).wait()
        v = p_ref.at[u, 0]
        pltpu.make_async_copy(v, v, zsend).wait()
        @pl.when(chan < 31)
        def _():
            carry_copy(u, chan + 1).wait_send()

NW = 256
def exchange(ci, win, x):
    V = pl.BlockSpec(memory_space=pltpu.VMEM)
    D = pltpu.SemaphoreType.DMA
    bf = jnp.bfloat16
    return pl.pallas_call(
        exchange_kernel, out_shape=jax.ShapeDtypeStruct((16, 192, 640), bf),
        in_specs=[V, pl.BlockSpec(memory_space=pl.ANY), pl.BlockSpec(memory_space=pl.ANY)], out_specs=V,
        scratch_shapes=[pltpu.VMEM((5, 3, 32, 32, 128), bf), pltpu.VMEM((1024, 128), jnp.float32), pltpu.VMEM((TAPS, N), jnp.float32),
                        pltpu.VMEM((2, 128, 3 * N), bf), pltpu.VMEM((256, N), bf), pltpu.VMEM((N, 512), bf), pltpu.VMEM((N, 512), bf),
                        pltpu.VMEM((2, 128, 512), jnp.float32), pltpu.VMEM((3, 2, 128, 512), bf), pltpu.VMEM((3, 2, 128, 512), bf),
                        pltpu.VMEM((3, 32, 32, 128), bf),
                        D, D, D((3,)), D((3,)), D, D((3, 8)), D, D((3,))],
        compiler_params=pltpu.CompilerParams(collective_id=0, has_side_effects=True, vmem_limit_bytes=58 * 2**20),
    )(ci.reshape(1, 512), win, x)

def keep_factor(flags_ref, keep_ref):
    own = lax.axis_index("stn")
    kept = (1 - flags_ref[...]).astype(jnp.float32).astype(jnp.bfloat16)
    pair = lax.broadcasted_iota(jnp.int32, (128, 64), 0) // 2 == lax.broadcasted_iota(jnp.int32, (128, 64), 1)
    pair = pair.astype(jnp.float32).astype(jnp.bfloat16)
    station = lax.broadcasted_iota(jnp.int32, (512, 128), 1) // 2
    for j in range(5):
        pick = lax.broadcasted_iota(jnp.int32, (512, 128), 0) == station + (own + 8 - j) % 8 * 64
        strip = jnp.dot(kept, pick.astype(jnp.float32).astype(jnp.bfloat16), preferred_element_type=jnp.float32)
        full = jnp.dot(pair, strip.astype(jnp.bfloat16), preferred_element_type=jnp.float32)
        keep_ref[:, j * 128:(j + 1) * 128] = full * (1.0 / 96)

def correlate_kernel(y_ref, flags_ref, out_ref, keep_ref):
    @pl.when(pl.program_id(0) == 0)
    def _():
        keep_factor(flags_ref, keep_ref)
    keep = keep_ref[...]
    for i in range(CH):
        cols = y_ref[i]
        rows = cols[:, :128]
        turned = jnp.concatenate([rows[96:], -rows[:96]], axis=0)
        both = jnp.concatenate([rows, turned], axis=1)
        sums = lax.dot_general(both, cols, (((0,), (0,)), ((), ())), preferred_element_type=jnp.float32)
        out_ref[i, 0] = (sums[:128] * keep).astype(jnp.bfloat16)
        out_ref[i, 1] = (sums[128:] * keep).astype(jnp.bfloat16)

CH = 4
def correlate(spectra, flags):
    return pl.pallas_call(
        correlate_kernel, grid=(16 // CH,), out_shape=jax.ShapeDtypeStruct((16, 2, 128, 640), jnp.bfloat16),
        in_specs=[pl.BlockSpec((CH, 192, 640), lambda i: (i, 0, 0)), pl.BlockSpec((64, 512), lambda i: (0, 0))],
        out_specs=pl.BlockSpec((CH, 2, 128, 640), lambda i: (i, 0, 0, 0)),
        scratch_shapes=[pltpu.VMEM((128, 640), jnp.float32)],
        compiler_params=pltpu.CompilerParams(vmem_limit_bytes=58 * 2**20),
    )(spectra, flags)

def on_device(samples, chan_index, flags):
    spectra = exchange(chan_index, jnp.asarray(window_np()), samples)
    return correlate(spectra, flags)

def solution(mesh):
    return jax.shard_map(on_device, mesh=mesh, in_specs=(P(None, "stn", "chan"), P(), P("stn", None)),
                         out_specs=P("chan", None, "stn", None), check_vma=False)
```

```python
import functools
import math

import jax
import jax.numpy as jnp
import numpy as np
from jax import lax
from jax.experimental import pallas as pl
from jax.experimental.pallas import tpu as pltpu
from jax.sharding import PartitionSpec as P

N = 4096
TAPS = 4

def window_np():
    pos = np.arange(TAPS * N, dtype=np.float64) + 0.5
    w = np.sinc(pos / N - TAPS / 2.0) * (0.5 - 0.5 * np.cos(2.0 * np.pi / (TAPS * N) * pos))
    w = w / np.sqrt(np.sum(w * w))
    return w.reshape(TAPS, N).astype(np.float32)

def cos_sin(q):
    quad = (q + 512) // 1024
    r = (q - quad * 1024).astype(jnp.float32) * (2.0 * math.pi / N)
    z = r * r
    s = r + r * z * (-1.0 / 6 + z * (1.0 / 120 + z * (-1.0 / 5040 + z * (1.0 / 362880))))
    c = 1.0 + z * (-0.5 + z * (1.0 / 24 + z * (-1.0 / 720 + z * (1.0 / 40320))))
    quad = quad & 3
    odd = (quad & 1) == 1
    cc = jnp.where(odd, s, c)
    ss = jnp.where(odd, c, s)
    cc = jnp.where((quad == 1) | (quad == 2), -cc, cc)
    ss = jnp.where(quad >= 2, -ss, ss)
    return cc, ss

ROWS = 64
def make_tables(ci_ref, tc_ref, ts_ref, lanes):
    for lc in lanes:
        for half in range(128 // ROWS):
            k = ci_ref[0:1, lc * 128:(lc + 1) * 128]
            k8 = jnp.broadcast_to(k, (8, 128))
            cd, sd = cos_sin((k8 * 128) & (N - 1))
            b = (lax.broadcasted_iota(jnp.int32, (ROWS // 8, 8, 128), 0) * 8
                 + lax.broadcasted_iota(jnp.int32, (ROWS // 8, 8, 128), 1) + half * ROWS)
            c, s = cos_sin((b * k8[None]) & (N - 1))
            def step(i, cs):
                c, s = cs
                row = pl.ds(pl.multiple_of(i * 128 + half * ROWS, ROWS), ROWS)
                tc_ref[row, lc * 128:(lc + 1) * 128] = c.reshape(ROWS, 128).astype(jnp.bfloat16)
                ts_ref[row, lc * 128:(lc + 1) * 128] = s.reshape(ROWS, 128).astype(jnp.bfloat16)
                return c * cd[None] - s * sd[None], s * cd[None] + c * sd[None]
            lax.fori_loop(0, N // 128, step, (c, s), unroll=2)

FT = 32
MESH = pl.DeviceIdType.MESH
UNITS = (2, 1, 0)

def signal(sem, dest):
    pl.semaphore_signal(sem, inc=1, device_id=dest, device_id_type=MESH)

def make_frames(u, carried, win_ref, x_ref, f_ref):
    def step(i, _):
        m0 = pl.multiple_of(i * 128, 128)
        w = [win_ref[p:p + 1, pl.ds(m0, 128)] for p in range(4)]
        segments = range(u, 3) if carried else range(u + 1)
        for r in range(2):
            for a in range(0, 128, FT):
                frame = 0.0
                for t in segments:
                    x = x_ref[r, a:a + FT, pl.ds(pl.multiple_of(t * N + m0, 128), 128)].astype(jnp.float32)
                    frame = frame + w[t - u if carried else 3 - u + t] * x
                f_ref[r * 128 + a:r * 128 + a + FT, pl.ds(m0, 128)] = frame.astype(jnp.bfloat16)
        return 0
    lax.fori_loop(0, N // 128, step, 0)

def relayout(j, u, g_ref, wide_ref, y_ref):
    lanes = pl.ds(pl.multiple_of(j * 128, 128), 128)
    wide_ref[...] = g_ref[j, u].reshape(1024, 128).astype(jnp.float32)
    for c in range(16):
        for r in range(2):
            k = (r * 3 + u) * 32
            y_ref[c, k:k + 32, lanes] = wide_ref[pl.ds(r * 16 + c, 32, stride=32), :].astype(jnp.bfloat16)

def half_dft(frame, tc_ref, ts_ref, n0, nw):
    pc = jnp.dot(frame, tc_ref[:, n0:n0 + nw], preferred_element_type=jnp.float32)
    ps = jnp.dot(frame, ts_ref[:, n0:n0 + nw], preferred_element_type=jnp.float32)
    return pc[:128] + ps[128:], pc[128:] - ps[:128]

def exchange_kernel(ci_ref, win_hbm, x_hbm, y_ref, g_ref, wide_ref, win_ref, x_ref, f_ref, tc_ref, ts_ref, main_ref, cout_ref, cin_ref, p_ref,
                    xsem, wsem, csend, crecv, zsend, zrecv, ysend, yrecv):
    chan, stn = lax.axis_index("chan"), lax.axis_index("stn")
    zl, x, core = chan // 8, (chan // 2) % 4, chan % 2
    zh, y = stn // 4, stn % 4
    late = y // 2

    xcopy = pltpu.make_async_copy(x_hbm, x_ref, xsem)
    xcopy.start()
    wcopy = pltpu.make_async_copy(win_hbm, win_ref, wsem)
    wcopy.start()

    barrier = pltpu.get_barrier_semaphore()
    def peer(n):
        far = (n // 32 + late) % 2
        q = (n // 8) % 4
        zz = (zl + 4 - q) % 4
        return zz * 8 + ((x + (n // 2) % 4) % 4) * 2 + (core + n) % 2, ((zh + far) % 2) * 4 + y, far
    def greet(n, _):
        c2, s2, far = peer(n)
        @pl.when(jnp.logical_or(c2 != chan, s2 != stn))
        def _():
            signal(barrier, (c2, s2))
        return 0
    lax.fori_loop(0, 64, greet, 0)
    def greet_y(d, _):
        signal(barrier, (chan, zh * 4 + (y + d) % 4))
        return 0
    lax.fori_loop(1, 4, greet_y, 0)

    make_tables(ci_ref, tc_ref, ts_ref, range(4))
    wcopy.wait()
    xcopy.wait()

    def carry_copy(u, h, dest):
        return pltpu.make_async_remote_copy(src_ref=cout_ref.at[u, h], dst_ref=cin_ref.at[u, h], send_sem=csend.at[u, h],
                                            recv_sem=crecv.at[u, h], device_id=(dest, stn), device_id_type=MESH)

    def keep_own(u):
        pltpu.make_async_copy(p_ref.at[u, chan], g_ref.at[0, u, chan], zrecv.at[u, zh * 4 + zl]).start()

    def send_batch(u, b):
        def send(n, _):
            c2, s2, far = peer(n)
            @pl.when(jnp.logical_or(c2 != chan, s2 != stn))
            def _():
                pltpu.make_async_remote_copy(
                    src_ref=p_ref.at[u, c2], dst_ref=g_ref.at[4 * far, u, chan], send_sem=zsend,
                    recv_sem=zrecv.at[u, zh * 4 + zl], device_id=(c2, s2), device_id_type=MESH).start()
            return 0
        lax.fori_loop(b * 8, b * 8 + 8, send, 0)

    def forward(u, n):
        far = (n // 4 + late) % 2
        zz = (zl + n) % 4
        v = g_ref.at[4 * far, u, pl.ds(zz * 8, 8)]
        pltpu.make_async_copy(v, v, zrecv.at[u, ((zh + far) % 2) * 4 + zz]).wait()
        for d in (2, 1, 3):
            @pl.when((y + d) // 4 == far)
            def _():
                pltpu.make_async_remote_copy(
                    src_ref=g_ref.at[4 * far, u, pl.ds(zz * 8, 8)], dst_ref=g_ref.at[d, u, pl.ds(zz * 8, 8)],
                    send_sem=ysend, recv_sem=yrecv.at[u], device_id=(chan, zh * 4 + (y + d) % 4),
                    device_id_type=MESH).start()

    def carried_part(u):
        make_frames(u, True, win_ref, x_ref, f_ref)
        for h in range(2):
            re, im = half_dft(f_ref[...], tc_ref, ts_ref, h * NW, NW)
            cout_ref[u, h, 0] = re.astype(jnp.bfloat16)
            cout_ref[u, h, 1] = im.astype(jnp.bfloat16)
            if u == UNITS[0] and h == 0:
                pl.semaphore_wait(barrier, 66)
            @pl.when(chan < 31)
            def _():
                carry_copy(u, h, chan + 1).start()

    def current_part(u):
        make_frames(u, False, win_ref, x_ref, f_ref)
        for n0 in range(0, 512, NW):
            re, im = half_dft(f_ref[...], tc_ref, ts_ref, n0, NW)
            main_ref[0, :, n0:n0 + NW] = re
            main_ref[1, :, n0:n0 + NW] = im

    def pieces(u):
        for h in range(2):
            @pl.when(chan == 0)
            def _():
                cin_ref[u, h] = jnp.zeros((2, 128, NW), jnp.bfloat16)
            @pl.when(chan > 0)
            def _():
                carry_copy(u, h, chan).wait_recv()
            for r in range(2):
                full = main_ref[r, :, h * NW:(h + 1) * NW] + cin_ref[u, h, r].astype(jnp.float32)
                for cb in range(2):
                    blk = full[:, cb * 128:(cb + 1) * 128].T.astype(jnp.bfloat16)
                    first_owner = h * 16 + cb * 8
                    p_ref[u, first_owner:first_owner + 8, r * 16:(r + 1) * 16, :] = blk.reshape(8, 16, 128)
        keep_own(u)

    def own_blocks(u):
        relayout(0, u, g_ref, wide_ref, y_ref)
        relayout(4, u, g_ref, wide_ref, y_ref)

    def other_blocks(u):
        v = g_ref.at[pl.ds(1, 3), u]
        pltpu.make_async_copy(v, v, yrecv.at[u]).wait()
        for j in range(1, 4):
            relayout(j, u, g_ref, wide_ref, y_ref)

    def steps(before, after, start, stop):
        def step(n, _):
            if before is not None:
                forward(before, n)
            if after is not None:
                send_batch(after, n)
            return 0
        lax.fori_loop(start, stop, step, 0)

    first, second, third = UNITS
    carried_part(first)
    current_part(first)
    pieces(first)
    steps(None, first, 0, 4)
    carried_part(second)
    steps(None, first, 4, 8)
    current_part(second)
    steps(first, None, 0, 3)
    carried_part(third)
    steps(first, None, 3, 5)
    pieces(second)
    steps(None, second, 0, 4)
    current_part(third)
    steps(first, None, 5, 6)
    steps(first, second, 6, 8)
    steps(None, second, 4, 6)
    pieces(third)
    steps(second, third, 0, 8)
    own_blocks(first)
    own_blocks(second)
    steps(third, None, 0, 8)
    other_blocks(first)
    own_blocks(third)
    other_blocks(second)
    other_blocks(third)
    for u in UNITS:
        v = g_ref.at[pl.ds(1, 3), u]
        pltpu.make_async_copy(v, v, ysend).wait()
        v = g_ref.at[pl.ds(0, 2), u, pl.ds(0, 31)]
        pltpu.make_async_copy(v, v, zsend).wait()
        v = p_ref.at[u, 0]
        pltpu.make_async_copy(v, v, zsend).wait()
        @pl.when(chan < 31)
        def _():
            for h in range(2):
                carry_copy(u, h, chan + 1).wait_send()

NW = 256
def exchange(ci, win, x):
    V = pl.BlockSpec(memory_space=pltpu.VMEM)
    D = pltpu.SemaphoreType.DMA
    bf = jnp.bfloat16
    return pl.pallas_call(
        exchange_kernel, out_shape=jax.ShapeDtypeStruct((16, 192, 640), bf),
        in_specs=[V, pl.BlockSpec(memory_space=pl.ANY), pl.BlockSpec(memory_space=pl.ANY)], out_specs=V,
        scratch_shapes=[pltpu.VMEM((5, 3, 32, 32, 128), bf), pltpu.VMEM((1024, 128), jnp.float32), pltpu.VMEM((TAPS, N), jnp.float32),
                        pltpu.VMEM((2, 128, 3 * N), bf), pltpu.VMEM((256, N), bf), pltpu.VMEM((N, 512), bf), pltpu.VMEM((N, 512), bf),
                        pltpu.VMEM((2, 128, 512), jnp.float32), pltpu.VMEM((3, 2, 2, 128, NW), bf), pltpu.VMEM((3, 2, 2, 128, NW), bf),
                        pltpu.VMEM((3, 32, 32, 128), bf),
                        D, D, D((3, 2)), D((3, 2)), D, D((3, 8)), D, D((3,))],
        compiler_params=pltpu.CompilerParams(collective_id=0, has_side_effects=True, vmem_limit_bytes=58 * 2**20),
    )(ci.reshape(1, 512), win, x)

def keep_factor(flags_ref, keep_ref):
    own = lax.axis_index("stn")
    kept = (1 - flags_ref[...]).astype(jnp.float32).astype(jnp.bfloat16)
    pair = lax.broadcasted_iota(jnp.int32, (128, 64), 0) // 2 == lax.broadcasted_iota(jnp.int32, (128, 64), 1)
    pair = pair.astype(jnp.float32).astype(jnp.bfloat16)
    station = lax.broadcasted_iota(jnp.int32, (512, 128), 1) // 2
    for j in range(5):
        pick = lax.broadcasted_iota(jnp.int32, (512, 128), 0) == station + (own + 8 - j) % 8 * 64
        strip = jnp.dot(kept, pick.astype(jnp.float32).astype(jnp.bfloat16), preferred_element_type=jnp.float32)
        full = jnp.dot(pair, strip.astype(jnp.bfloat16), preferred_element_type=jnp.float32)
        keep_ref[:, j * 128:(j + 1) * 128] = full * (1.0 / 96)

def correlate_kernel(y_ref, flags_ref, out_ref, keep_ref):
    @pl.when(pl.program_id(0) == 0)
    def _():
        keep_factor(flags_ref, keep_ref)
    keep = keep_ref[...]
    for i in range(CH):
        cols = y_ref[i]
        rows = cols[:, :128]
        turned = jnp.concatenate([rows[96:], -rows[:96]], axis=0)
        both = jnp.concatenate([rows, turned], axis=1)
        sums = lax.dot_general(both, cols, (((0,), (0,)), ((), ())), preferred_element_type=jnp.float32)
        out_ref[i, 0] = (sums[:128] * keep).astype(jnp.bfloat16)
        out_ref[i, 1] = (sums[128:] * keep).astype(jnp.bfloat16)

CH = 4
def correlate(spectra, flags):
    return pl.pallas_call(
        correlate_kernel, grid=(16 // CH,), out_shape=jax.ShapeDtypeStruct((16, 2, 128, 640), jnp.bfloat16),
        in_specs=[pl.BlockSpec((CH, 192, 640), lambda i: (i, 0, 0)), pl.BlockSpec((64, 512), lambda i: (0, 0))],
        out_specs=pl.BlockSpec((CH, 2, 128, 640), lambda i: (i, 0, 0, 0)),
        scratch_shapes=[pltpu.VMEM((128, 640), jnp.float32)],
        compiler_params=pltpu.CompilerParams(vmem_limit_bytes=58 * 2**20),
    )(spectra, flags)

def on_device(samples, chan_index, flags):
    spectra = exchange(chan_index, jnp.asarray(window_np()), samples)
    return correlate(spectra, flags)

def solution(mesh):
    return jax.shard_map(on_device, mesh=mesh, in_specs=(P(None, "stn", "chan"), P(), P("stn", None)),
                         out_specs=P("chan", None, "stn", None), check_vma=False)
```
